32 devices in a mesh: group: 2 (over x), tile: 16 (over z, y, core).
Axes of the slice: x: 2, y: 2, z: 4, core: 2. Of those that a mesh axis runs over, the one named last changes fastest.
Arguments:
- east_wind: float32 [2, 8, 256, 2048], P('group', None, 'tile'), may hold values from -6 to 6
- equator_wind: float32 [2, 8, 256, 2048], P('group', None, 'tile'), may hold values from -6 to 6
- pressure: float32 [2, 8, 256, 2048], P('group', None, 'tile'), may hold values from -6 to 6
- moisture: float32 [2, 8, 256, 2048], P('group', None, 'tile'), may hold values from 0.05 to 0.5
- albedo: float32 [2, 256, 2048], P('group', 'tile'), may hold values from 0.05 to 0.8
- courant: float32 [8], replicated, may hold values from 0.3 to 1.2
- sun_angles: float32 [2], replicated, may hold values from -3.140625 to 3.140625
- absorption: float32 [256], replicated, may hold values from 0.01 to 30
- solar_weights: float32 [256], replicated, may hold values from 0.05 to 5
Outputs:
- east_wind_next: float32 [2, 8, 256, 2048], P('group', None, 'tile')
- equator_wind_next: float32 [2, 8, 256, 2048], P('group', None, 'tile')
- pressure_next: float32 [2, 8, 256, 2048], P('group', None, 'tile')
The draws below stay inside these ranges and needn't reach their ends.
All inputs are finite; a program needn't handle non-finite values.
Results may differ from the reference program's by a relative error of at most 0.0001.
Values sent between devices are 32-bit elements; how exact they have to be, the bound alone decides.
A program may use at most 128 MiB of HBM per device.

```python
import math
import jax
import jax.numpy as jnp
from jax import lax

LEV = 8
G = 256
SUB = 6
NYH = 256
NX = 2048


def levels(key, dims, pieces, smallest, high):
    gain, own = 1.0, jax.random.fold_in(key, 6)
    for axis_at, shards_of in pieces:
        heights = jnp.exp(jax.random.uniform(jax.random.fold_in(own, axis_at), (shards_of,), jnp.float32, smallest / len(pieces), high / len(pieces)))
        gain = gain * jnp.repeat(heights, dims[axis_at] // shards_of).reshape([-1 if axis == axis_at else 1 for axis in range(len(dims))])
    return gain


def normal_values(key, dims, width, reach, pieces=(), kind=jnp.bfloat16):
    gain = levels(key, dims, pieces, -0.22, 0.18) if pieces else 1.0
    result = jax.random.normal(key, dims, jnp.float32) * width * gain
    return jnp.minimum(jnp.maximum(result, -reach), reach).astype(kind)


def setup_inputs(seed: int = 0) -> dict:
    splits = jax.random.split(jax.random.key(seed), 10)
    return {
        "east_wind": normal_values(splits[0], (2, LEV, NYH, NX), 1.0, 6.0, ((0, 2), (2, 16)), jnp.float32),
        "equator_wind": normal_values(splits[1], (2, LEV, NYH, NX), 1.0, 6.0, ((0, 2), (2, 16)), jnp.float32),
        "pressure": normal_values(splits[2], (2, LEV, NYH, NX), 1.0, 6.0, ((0, 2), (2, 16)), jnp.float32),
        "moisture": jnp.clip(0.05 + 0.45 * jax.random.uniform(splits[3], (2, LEV, NYH, NX), jnp.float32) ** levels(splits[3], (2, LEV, NYH, NX), ((0, 2), (2, 16)), -0.2, 0.2), 0.05, 0.5),
        "albedo": jnp.clip(0.05 + 0.75 * jax.random.uniform(splits[4], (2, NYH, NX), jnp.float32) ** levels(splits[4], (2, NYH, NX), ((0, 2), (1, 16)), -0.2, 0.2), 0.05, 0.8),
        "courant": jnp.clip(jnp.exp(jax.random.uniform(splits[5], (LEV,), jnp.float32, math.log(0.3), math.log(1.2))), 0.3, 1.2),
        "sun_angles": jnp.clip(jax.random.uniform(splits[6], (2,), jnp.float32, -3.140625, 3.140625), -3.140625, 3.140625),
        "absorption": jnp.clip(jnp.exp(jax.random.uniform(splits[7], (G,), jnp.float32, math.log(0.01), math.log(30.0))), 0.01, 30.0),
        "solar_weights": jnp.clip(jnp.exp(jax.random.uniform(splits[8], (G,), jnp.float32, math.log(0.05), math.log(5.0))), 0.05, 5.0),
    }


HEAT_SCALE = 10.0
MU_OFFSET = 0.1
DIFFUSE = 1.66


def centred_rows(values, mirror_sign):
    pole_rim = jnp.zeros_like(values[:, :, :1, :])
    equator = mirror_sign * values[::-1, :, -1:, :]
    extended = jnp.concatenate([pole_rim, values, equator], axis=2)
    return extended[:, :, 2:, :], extended[:, :, :-2, :]


def radiate(absorber, sun_cos, surface, absorption, solar_weights):
    sunlit = jnp.maximum(sun_cos, 0.0)
    slant_path = 1.0 / (sunlit + MU_OFFSET)
    optical_depth = jnp.concatenate([jnp.zeros_like(absorber[:1]), jnp.cumsum(absorber, axis=0)], axis=0)
    column_depth = optical_depth[-1:]
    coeffs = absorption.reshape((-1,) + (1,) * optical_depth.ndim)
    down_flux = jnp.exp(-coeffs * (optical_depth * slant_path))
    up_flux = jnp.exp(-coeffs * (column_depth * slant_path + DIFFUSE * (column_depth - optical_depth)))
    weights = (solar_weights / solar_weights.shape[0]).reshape(coeffs.shape)
    net_flux = jnp.sum(weights * (down_flux - surface * up_flux), axis=0) * sunlit
    return HEAT_SCALE * (net_flux[:-1] - net_flux[1:])


def sun_cosine(latitude, longitude, sun_angles):
    declination = 0.41 * jnp.sin(sun_angles[0])
    return (jnp.sin(latitude)[:, None] * jnp.sin(declination)
            + jnp.cos(latitude)[:, None] * jnp.cos(declination) * jnp.cos(longitude[None, :] - sun_angles[1]))


def reference(east_wind, equator_wind, pressure, moisture, albedo, courant, sun_angles, absorption, solar_weights):
    courant_col = courant[None, :, None, None]
    for substep in range(SUB):
        ahead_wind, behind_wind = centred_rows(equator_wind, -1.0)
        divergence = 0.5 * (jnp.roll(east_wind, -1, 3) - jnp.roll(east_wind, 1, 3) + ahead_wind - behind_wind)
        pressure = pressure - courant_col * divergence
        ahead_press, behind_press = centred_rows(pressure, 1.0)
        east_wind = east_wind - courant_col * (0.5 * (jnp.roll(pressure, -1, 3) - jnp.roll(pressure, 1, 3)))
        equator_wind = equator_wind - courant_col * (0.5 * (ahead_press - behind_press))
    half_rows = NYH // 2
    half_cols = NX // 2
    coarse_moist = moisture.reshape(2, LEV, half_rows, 2, half_cols, 2).mean(axis=(3, 5))
    coarse_albedo = albedo.reshape(2, half_rows, 2, half_cols, 2).mean(axis=(2, 4))
    colatitude = 1.0 - (jnp.arange(half_rows).astype(jnp.float32) + 0.5) / half_rows
    longitude = 2.0 * jnp.pi * (jnp.arange(half_cols).astype(jnp.float32) + 0.5) / half_cols

    def one_row(packed):
        absorber_row, sun_row, surface_row = packed
        return radiate(absorber_row, sun_row, surface_row, absorption, solar_weights)

    heat_parts = []
    for hemisphere in range(2):
        sign_value = 2.0 * hemisphere - 1.0
        latitude = sign_value * (0.5 * jnp.pi) * colatitude
        sun_cos = sun_cosine(latitude, longitude, sun_angles)
        absorber_rows = jnp.moveaxis(coarse_moist[hemisphere], 1, 0)
        heat_rows = lax.map(one_row, (absorber_rows, sun_cos, coarse_albedo[hemisphere]))
        heat_parts.append(jnp.moveaxis(heat_rows, 0, 1))
    heating = jnp.stack(heat_parts)
    fine_heat = jnp.repeat(jnp.repeat(heating, 2, axis=2), 2, axis=3)
    return east_wind, equator_wind, pressure + fine_heat
```

```python
import functools
import math

import jax
import jax.numpy as jnp
from jax import lax
from jax.experimental import pallas as pl
from jax.experimental.pallas import tpu as pltpu
from jax.sharding import PartitionSpec as P

SUB = 6
HEAT_SCALE = 10.0
MU_OFFSET = 0.1
DIFFUSE = 1.66
LOG2E = math.log2(math.e)
CHUNK = 4
OFF = 8


def wide(vec, cols):
    return jnp.concatenate([vec] * (cols // vec.shape[1]), axis=1)


def msg_rows(n):
    return (1 + 2 * (n - 1), 1 if n == SUB else 2)


def part_rows(n):
    first, count = msg_rows(n)
    return (0, 3) if n == 1 else (first, count)


def cone(n, rows):
    low = max(-1 - 2 * (n - 1), -1 - 2 * (SUB - n))
    return low, min(2 * (SUB - n), rows - 1)


def kernel(
    tiles,
    east, equator, press, moist, alb, courant, sun, absorb, weights,
    east_out, equator_out, press_out,
    u_s, v_s, p_s, m_s, a_s, d0, pa, pb, acc, heat, lat_s, lon_s, tau, fsum,
    xa, xb, xd, keep, send, recv,
    in_sem, out_sem, send_sem, recv_sem,
):
    rows, levels, cols = p_s.shape
    g, t = lax.axis_index("group"), lax.axis_index("tile")
    last = (t + 1) // tiles
    down = (g + last * (1 - 2 * g), t + 1 - last)
    mesh_ids = pl.DeviceIdType.MESH

    barrier = pltpu.get_barrier_semaphore()
    pl.semaphore_signal(barrier, inc=1, device_id=down, device_id_type=mesh_ids)

    @pl.when(t > 0)
    def _():
        pl.semaphore_signal(barrier, inc=1, device_id=(g, t - 1), device_id_type=mesh_ids)

    def loads(r):
        return [
            pltpu.make_async_copy(press.at[0, :, r, :], p_s.at[r], in_sem.at[0]),
            pltpu.make_async_copy(east.at[0, :, r, :], u_s.at[r], in_sem.at[1]),
            pltpu.make_async_copy(equator.at[0, :, r, :], v_s.at[r + 1], in_sem.at[2]),
        ]

    for r in range(rows):
        for c in loads(r):
            c.start()
    for r in range(rows):
        pltpu.make_async_copy(moist.at[0, :, r, :], m_s.at[r], in_sem.at[3]).start()
    for b in range(cols // 128):
        pltpu.make_async_copy(
            alb.at[0, :, pl.ds(b * 128, 128)], a_s.at[b], in_sem.at[4]
        ).start()

    lane = lax.broadcasted_iota(jnp.int32, (levels, 128), 1)
    sub = lax.broadcasted_iota(jnp.int32, (levels, 128), 0)
    even = lane % 2 == 0
    cvec = jnp.zeros((levels, 128), jnp.float32)
    for l in range(levels):
        cvec = jnp.where(sub == l, courant[l], cvec)
    half_c = wide(0.5 * cvec, cols)
    kappa = wide(0.25 * cvec * cvec, cols)

    zero_row = jnp.zeros((levels, cols), jnp.float32)
    v_s[0] = zero_row
    v_s[rows + 1] = zero_row
    for s in (0, 1):
        for q in range(-7, -1):
            xa[s, OFF + q] = zero_row
            xb[s, OFF + q] = zero_row
            xd[s, OFF + q] = zero_row

    for c, dst in ((0, p_s), (1, u_s), (2, v_s.at[pl.ds(1, rows)])):
        pltpu.make_async_copy(dst, dst, in_sem.at[c]).wait()

    def roll(x, by):
        return pltpu.roll(x, by % cols, 1)

    def div_row(r, _):
        u = u_s[r]
        d0[r] = half_c * (roll(u, -1) - roll(u, 1) + v_s[r + 2] - v_s[r])
        return 0

    lax.fori_loop(0, rows, div_row, 0)

    edge0 = half_c * v_s[1]
    edge1 = -half_c * v_s[rows]
    for s, e in ((0, edge0), (1, edge1)):
        send[s, 0] = e
        xd[s, OFF - 1] = e
        xa[s, OFF - 1] = -e

    def start_row(q, _):
        for s, r in ((0, q), (1, rows - 1 - q)):
            d = d0[r]
            xd[s, OFF + q] = d
            xa[s, OFF + q] = p_s[r] - d
        return 0

    lax.fori_loop(0, cone(1, rows)[1] + 1, start_row, 0)

    def up_copy(n):
        first, count = part_rows(n)
        return pltpu.make_async_remote_copy(
            src_ref=send.at[0, pl.ds(first, count)],
            dst_ref=recv.at[1, pl.ds(first, count)],
            send_sem=send_sem.at[0, n - 1],
            recv_sem=recv_sem.at[1, n - 1],
            device_id=(g, t - 1),
            device_id_type=mesh_ids,
        )

    def down_copy(n):
        first, count = part_rows(n)
        return pltpu.make_async_remote_copy(
            src_ref=send.at[1, pl.ds(first, count)],
            dst_ref=recv.at[last, pl.ds(first, count)],
            send_sem=send_sem.at[1, n - 1],
            recv_sem=recv_sem.at[last, n - 1],
            device_id=down,
            device_id_type=mesh_ids,
        )

    def recv_copy(s, n):
        first, count = part_rows(n)
        return pltpu.make_async_copy(
            recv.at[s, pl.ds(first, count)], recv.at[s, pl.ds(first, count)], recv_sem.at[s, n - 1]
        )

    def laplace(x, x_low, x_high):
        return roll(x, 2) + roll(x, -2) + x_low + x_high - 4.0 * x

    cur, nxt = xa, xb
    for n in range(1, SUB + 1):
        if n > 1:
            low, high = cone(n, rows)

            def strip_row(i, _, cur=cur, nxt=nxt):
                for s in (0, 1):
                    x = cur[s, i]
                    d = xd[s, i] - kappa * laplace(x, cur[s, i - 2], cur[s, i + 2])
                    xd[s, i] = d
                    nxt[s, i] = x - d
                return 0

            lax.fori_loop(OFF + low, OFF + high + 1, strip_row, 0)
            cur, nxt = nxt, cur
        first, count = msg_rows(n)
        for s in (0, 1):
            for j in range(count):
                send[s, first + j] = cur[s, OFF + j]
                keep[s, first + j] = cur[s, OFF - 1 - j]
        if n == 1:
            pl.semaphore_wait(barrier, 1 + (t + tiles - 1) // tiles)
        down_copy(n).start()

        @pl.when(t > 0)
        def _(n=n):
            up_copy(n).start()

    half_rows = rows // 2
    quads = rows // 4
    blocks = cols // 128
    dec = 0.41 * jnp.sin(jnp.full((8, 128), sun[0], jnp.float32))
    sin_dec, cos_dec = jnp.sin(dec)[:levels], jnp.cos(dec)[:levels]
    krow = lax.broadcasted_iota(jnp.int32, (half_rows, 128), 0) + t * half_rows
    colat = 1.0 - (krow.astype(jnp.float32) + 0.5) / (tiles * half_rows)
    lat = (2.0 * g.astype(jnp.float32) - 1.0) * (0.5 * jnp.pi) * colat
    lat_s[0] = jnp.sin(lat)
    lat_s[1] = jnp.cos(lat)
    col = lax.broadcasted_iota(jnp.int32, (1, cols), 1) // 2
    lon = 2.0 * jnp.pi * (col.astype(jnp.float32) + 0.5) / (cols // 2)
    lon_s[...] = jnp.cos(lon - jnp.full((1, cols), sun[1], jnp.float32))
    pltpu.make_async_copy(m_s, m_s, in_sem.at[3]).wait()
    pltpu.make_async_copy(a_s, a_s, in_sem.at[4]).wait()

    def pair(x, y):
        return 0.25 * jnp.where(
            even, x + pltpu.roll(x, 127, 1), y + pltpu.roll(y, 1, 1)
        )

    def sunlit_of(m, b):
        def lat_row(i, k):
            return jnp.broadcast_to(lat_s[i, pl.ds(k, 1), :], (levels, 128))

        sl = jnp.where(even, lat_row(0, 2 * m), lat_row(0, 2 * m + 1))
        cl = jnp.where(even, lat_row(1, 2 * m), lat_row(1, 2 * m + 1))
        coslon = jnp.broadcast_to(lon_s[:, b * 128:(b + 1) * 128], (levels, 128))
        return jnp.maximum(sl * sin_dec + cl * cos_dec * coslon, 0.0)

    def prepare(m, _):
        for b in range(blocks):
            at = pl.ds(b * 128, 128)
            x = pair(
                m_s[4 * m, :, at] + m_s[4 * m + 1, :, at],
                m_s[4 * m + 2, :, at] + m_s[4 * m + 3, :, at],
            )
            depth = x
            for step in (1, 2, 4):
                depth = depth + jnp.where(sub >= step, pltpu.roll(depth, step, 0), 0.0)
            above = jnp.where(sub >= 1, pltpu.roll(depth, 1, 0), 0.0)
            total = jnp.broadcast_to(depth[levels - 1:levels, :], (levels, 128))
            slant = 1.0 / (sunlit_of(m, b) + MU_OFFSET)
            i = m * blocks + b
            tau[2 * i] = -LOG2E * (depth * slant)
            tau[2 * i + 1] = -LOG2E * (total * slant + DIFFUSE * (total - above))
        return 0

    lax.fori_loop(0, quads, prepare, 0)

    gpoints = absorb.shape[0]
    unroll = 4

    def fluxes(j, _):
        taus = [tau[j * 2 * CHUNK + i] for i in range(2 * CHUNK)]

        def gstep(h, sums):
            for e in range(unroll):
                a, w = absorb[h * unroll + e], weights[h * unroll + e]
                sums = tuple(s + w * jnp.exp2(a * x) for s, x in zip(sums, taus))
            return sums

        zeros = tuple(jnp.zeros((levels, 128), jnp.float32) for _ in taus)
        sums = lax.fori_loop(0, gpoints // unroll, gstep, zeros)
        for i in range(2 * CHUNK):
            fsum[j * 2 * CHUNK + i] = sums[i]
        return 0

    lax.fori_loop(0, quads * blocks // CHUNK, fluxes, 0)

    wsum = lax.fori_loop(0, gpoints, lambda h, s: s + weights[h], jnp.float32(0.0))
    top = jnp.full((levels, 128), wsum, jnp.float32)
    scale = HEAT_SCALE / gpoints

    def heat_row(m, _):
        for b in range(blocks):
            at = pl.ds(b * 128, 128)

            def alb_row(r):
                return jnp.broadcast_to(a_s[b, pl.ds(4 * m + r, 1), :], (levels, 128))

            surface = pair(alb_row(0) + alb_row(1), alb_row(2) + alb_row(3))
            i = m * blocks + b
            fd, fu = fsum[2 * i], fsum[2 * i + 1]
            fd_above = jnp.where(sub == 0, top, pltpu.roll(fd, 1, 0))
            fu_below = jnp.where(sub == levels - 1, fd, pltpu.roll(fu, levels - 1, 0))
            h = scale * sunlit_of(m, b) * ((fd_above - fd) - surface * (fu - fu_below))
            heat[2 * m, :, at] = jnp.where(even, h, pltpu.roll(h, 1, 1))
            heat[2 * m + 1, :, at] = jnp.where(even, pltpu.roll(h, 127, 1), h)
        return 0

    lax.fori_loop(0, quads, heat_row, 0)

    def halo(n, dst):
        first, count = msg_rows(n)

        @pl.when(t > 0)
        def _():
            recv_copy(0, n).wait()

        recv_copy(1, n).wait()
        if n == 1:
            @pl.when(t > 0)
            def _():
                e = recv[0, 0]
                d0[0] = d0[0] + e
                dst[2] = dst[2] - e
                acc[1] = acc[1] - e
            e = recv[1, 0]
            d0[rows - 1] = d0[rows - 1] + e
            dst[rows + 1] = dst[rows + 1] - e
            acc[rows] = acc[rows] - e

        for j in range(count):
            dst[rows + 2 + j] = recv[1, first + j] + keep[1, first + j]

        @pl.when(t > 0)
        def _():
            for j in range(count):
                dst[1 - j] = recv[0, first + j] + keep[0, first + j]

        @pl.when(t == 0)
        def _():
            dst[1] = zero_row
            if count > 1:
                dst[0] = dst[2]

        if n == 1:
            acc[0] = dst[1]
            acc[rows + 1] = dst[rows + 2]
        else:
            acc[0] = acc[0] + dst[1]
            acc[rows + 1] = acc[rows + 1] + dst[rows + 2]

    def first_row(r, _):
        x = p_s[r] - d0[r]
        pa[r + 2] = x
        acc[r + 1] = x
        return 0

    lax.fori_loop(0, rows, first_row, 0)
    cur, nxt = pa, pb
    halo(1, cur)
    for n in range(2, SUB + 1):
        def full_row(r, _, cur=cur, nxt=nxt):
            x = cur[r + 2]
            d = d0[r] - kappa * laplace(x, cur[r], cur[r + 4])
            x = x - d
            d0[r] = d
            nxt[r + 2] = x
            acc[r + 1] = acc[r + 1] + x
            return 0

        lax.fori_loop(0, rows, full_row, 0)
        cur, nxt = nxt, cur
        halo(n, cur)

    def final_row(r, _, cur=cur):
        x = acc[r + 1]
        u_s[r] = u_s[r] - half_c * (roll(x, -1) - roll(x, 1))
        v_s[r + 1] = v_s[r + 1] - half_c * (acc[r + 2] - acc[r])
        p_s[r] = cur[r + 2] + heat[r // 2]
        return 0

    lax.fori_loop(0, rows, final_row, 0)
    outs = [
        pltpu.make_async_copy(p_s, press_out, out_sem.at[0]),
        pltpu.make_async_copy(u_s, east_out, out_sem.at[1]),
        pltpu.make_async_copy(v_s.at[pl.ds(1, rows)], equator_out, out_sem.at[2]),
    ]
    for c in outs:
        c.start()
    for n in range(1, SUB + 1):
        down_copy(n).wait_send()

        @pl.when(t > 0)
        def _(n=n):
            up_copy(n).wait_send()
    for c in outs:
        c.wait()


def shards(tiles, east, equator, press, moist, alb, courant, sun, absorb, weights):
    _, levels, rows, cols = press.shape
    half_rows, quads, blocks = rows // 2, rows // 4, cols // 128
    row = lambda *lead: pltpu.VMEM(lead + (levels, cols), jnp.float32)
    out = jax.ShapeDtypeStruct((rows, levels, cols), jnp.float32)
    hbm = pl.BlockSpec(memory_space=pl.ANY)
    smem = pl.BlockSpec(memory_space=pltpu.SMEM)
    outs = pl.pallas_call(
        functools.partial(kernel, tiles),
        out_shape=(out, out, out),
        in_specs=[hbm] * 5 + [smem] * 4,
        out_specs=(hbm, hbm, hbm),
        scratch_shapes=[
            row(rows), row(rows + 2), row(rows), row(rows),
            pltpu.VMEM((blocks, rows, 128), jnp.float32),
            row(rows), row(rows + 4), row(rows + 4), row(rows + 2), row(half_rows),
            pltpu.VMEM((2, half_rows, 128), jnp.float32),
            pltpu.VMEM((1, cols), jnp.float32),
            pltpu.VMEM((2 * quads * blocks, levels, 128), jnp.float32),
            pltpu.VMEM((2 * quads * blocks, levels, 128), jnp.float32),
            row(2, OFF + rows), row(2, OFF + rows), row(2, OFF + rows),
            row(2, 2 * SUB), row(2, 2 * SUB), row(2, 2 * SUB),
            pltpu.SemaphoreType.DMA((5,)),
            pltpu.SemaphoreType.DMA((3,)),
            pltpu.SemaphoreType.DMA((2, SUB)),
            pltpu.SemaphoreType.DMA((2, SUB)),
        ],
        compiler_params=pltpu.CompilerParams(
            collective_id=0, has_side_effects=True, vmem_limit_bytes=56 * 1024 * 1024
        ),
        name="step",
    )(east, equator, press, moist, alb, courant, sun, absorb, weights)
    return tuple(jnp.swapaxes(o, 0, 1)[None] for o in outs)


def solution(mesh):
    field = P("group", None, "tile", None)
    return jax.shard_map(
        functools.partial(shards, mesh.shape["tile"]),
        mesh=mesh,
        in_specs=(field, field, field, field, P("group", "tile", None), P(), P(), P(), P()),
        out_specs=(field, field, field),
        check_vma=False,
    )
```

```python
import functools
import math

import jax
import jax.numpy as jnp
from jax import lax
from jax.experimental import pallas as pl
from jax.experimental.pallas import tpu as pltpu
from jax.sharding import PartitionSpec as P

SUB = 6
HEAT_SCALE = 10.0
MU_OFFSET = 0.1
DIFFUSE = 1.66
LOG2E = math.log2(math.e)
CHUNK = 8
OFF = 8


def wide(vec, cols):
    return jnp.concatenate([vec] * (cols // vec.shape[1]), axis=1)


def msg_rows(n):
    return (1 + 2 * (n - 1), 1 if n == SUB else 2)


def part_rows(n):
    first, count = msg_rows(n)
    return (0, 3) if n == 1 else (first, count)


def cone(n, rows):
    low = max(-1 - 2 * (n - 1), -1 - 2 * (SUB - n))
    return low, min(2 * (SUB - n), rows - 1)


def kernel(
    tiles,
    east, equator, press, moist, alb, courant, sun, absorb, weights,
    east_out, equator_out, press_out,
    u_s, v_s, p_s, m_s, a_s, d0, pa, pb, acc, heat, lat_s, lon_s, tau, fsum,
    xa, xb, xd, keep, send, recv,
    in_sem, out_sem, send_sem, recv_sem,
):
    rows, levels, cols = p_s.shape
    g, t = lax.axis_index("group"), lax.axis_index("tile")
    last = (t + 1) // tiles
    down = (g + last * (1 - 2 * g), t + 1 - last)
    mesh_ids = pl.DeviceIdType.MESH

    barrier = pltpu.get_barrier_semaphore()
    pl.semaphore_signal(barrier, inc=1, device_id=down, device_id_type=mesh_ids)

    @pl.when(t > 0)
    def _():
        pl.semaphore_signal(barrier, inc=1, device_id=(g, t - 1), device_id_type=mesh_ids)

    def loads(r):
        return [
            pltpu.make_async_copy(press.at[0, :, r, :], p_s.at[r], in_sem.at[0]),
            pltpu.make_async_copy(east.at[0, :, r, :], u_s.at[r], in_sem.at[1]),
            pltpu.make_async_copy(equator.at[0, :, r, :], v_s.at[r + 1], in_sem.at[2]),
        ]

    for r in range(rows):
        for c in loads(r):
            c.start()
    for r in range(rows):
        pltpu.make_async_copy(moist.at[0, :, r, :], m_s.at[r], in_sem.at[3]).start()
    for b in range(cols // 128):
        pltpu.make_async_copy(
            alb.at[0, :, pl.ds(b * 128, 128)], a_s.at[b], in_sem.at[4]
        ).start()

    lane = lax.broadcasted_iota(jnp.int32, (levels, 128), 1)
    sub = lax.broadcasted_iota(jnp.int32, (levels, 128), 0)
    even = lane % 2 == 0
    cvec = jnp.zeros((levels, 128), jnp.float32)
    for l in range(levels):
        cvec = jnp.where(sub == l, courant[l], cvec)
    half_c = wide(0.5 * cvec, cols)

    zero_row = jnp.zeros((levels, cols), jnp.float32)
    v_s[0] = zero_row
    v_s[rows + 1] = zero_row
    for s in (0, 1):
        for q in range(-7, -1):
            xa[s, OFF + q] = zero_row
            xb[s, OFF + q] = zero_row
            xd[s, OFF + q] = zero_row

    for c, dst in ((0, p_s), (1, u_s), (2, v_s.at[pl.ds(1, rows)])):
        pltpu.make_async_copy(dst, dst, in_sem.at[c]).wait()

    def roll(x, by):
        return pltpu.roll(x, by % cols, 1)

    def div_row(r, _):
        u = u_s[r]
        d0[r] = half_c * (roll(u, -1) - roll(u, 1) + v_s[r + 2] - v_s[r])
        return 0

    lax.fori_loop(0, rows, div_row, 0)

    edge0 = half_c * v_s[1]
    edge1 = -half_c * v_s[rows]
    for s, e in ((0, edge0), (1, edge1)):
        send[s, 0] = e
        xd[s, OFF - 1] = e
        xa[s, OFF - 1] = -e

    def start_row(q, _):
        for s, r in ((0, q), (1, rows - 1 - q)):
            d = d0[r]
            xd[s, OFF + q] = d
            xa[s, OFF + q] = p_s[r] - d
        return 0

    lax.fori_loop(0, cone(1, rows)[1] + 1, start_row, 0)

    def up_copy(n):
        first, count = part_rows(n)
        return pltpu.make_async_remote_copy(
            src_ref=send.at[0, pl.ds(first, count)],
            dst_ref=recv.at[1, pl.ds(first, count)],
            send_sem=send_sem.at[0, n - 1],
            recv_sem=recv_sem.at[1, n - 1],
            device_id=(g, t - 1),
            device_id_type=mesh_ids,
        )

    def down_copy(n):
        first, count = part_rows(n)
        return pltpu.make_async_remote_copy(
            src_ref=send.at[1, pl.ds(first, count)],
            dst_ref=recv.at[last, pl.ds(first, count)],
            send_sem=send_sem.at[1, n - 1],
            recv_sem=recv_sem.at[last, n - 1],
            device_id=down,
            device_id_type=mesh_ids,
        )

    def recv_copy(s, n):
        first, count = part_rows(n)
        return pltpu.make_async_copy(
            recv.at[s, pl.ds(first, count)], recv.at[s, pl.ds(first, count)], recv_sem.at[s, n - 1]
        )

    kap = 0.25 * cvec * cvec
    cols_of = [pl.ds(b * 128, 128) for b in range(cols // 128)]

    def row_step(x_ref, low_ref, high_ref, d_ref, new_ref, sum_ref=None):
        xs = [x_ref[:, at] for at in cols_of]
        ahead = [pltpu.roll(x, 126, 1) for x in xs]
        behind = [pltpu.roll(x, 2, 1) for x in xs]
        for b, at in enumerate(cols_of):
            west = jnp.where(lane < 2, behind[b - 1], behind[b])
            east_x = jnp.where(lane >= 126, ahead[(b + 1) % len(xs)], ahead[b])
            lap = (west + east_x) + (low_ref[:, at] + high_ref[:, at]) - 4.0 * xs[b]
            d = d_ref[:, at] - kap * lap
            x = xs[b] - d
            d_ref[:, at] = d
            new_ref[:, at] = x
            if sum_ref is not None:
                sum_ref[:, at] = sum_ref[:, at] + x

    cur, nxt = xa, xb
    for n in range(1, SUB + 1):
        if n > 1:
            low, high = cone(n, rows)

            def strip_row(i, _, cur=cur, nxt=nxt):
                for s in (0, 1):
                    row_step(cur.at[s, i], cur.at[s, i - 2], cur.at[s, i + 2], xd.at[s, i], nxt.at[s, i])
                return 0

            lax.fori_loop(OFF + low, OFF + high + 1, strip_row, 0)
            cur, nxt = nxt, cur
        first, count = msg_rows(n)
        for s in (0, 1):
            for j in range(count):
                send[s, first + j] = cur[s, OFF + j]
                keep[s, first + j] = cur[s, OFF - 1 - j]
        if n == 1:
            pl.semaphore_wait(barrier, 1 + (t + tiles - 1) // tiles)
        down_copy(n).start()

        @pl.when(t > 0)
        def _(n=n):
            up_copy(n).start()

    half_rows = rows // 2
    quads = rows // 4
    blocks = cols // 128
    dec = 0.41 * jnp.sin(jnp.full((8, 128), sun[0], jnp.float32))
    sin_dec, cos_dec = jnp.sin(dec)[:levels], jnp.cos(dec)[:levels]
    krow = lax.broadcasted_iota(jnp.int32, (half_rows, 128), 0) + t * half_rows
    colat = 1.0 - (krow.astype(jnp.float32) + 0.5) / (tiles * half_rows)
    lat = (2.0 * g.astype(jnp.float32) - 1.0) * (0.5 * jnp.pi) * colat
    lat_s[0] = jnp.sin(lat)
    lat_s[1] = jnp.cos(lat)
    col = lax.broadcasted_iota(jnp.int32, (1, cols), 1) // 2
    lon = 2.0 * jnp.pi * (col.astype(jnp.float32) + 0.5) / (cols // 2)
    lon_s[...] = jnp.cos(lon - jnp.full((1, cols), sun[1], jnp.float32))
    pltpu.make_async_copy(m_s, m_s, in_sem.at[3]).wait()
    pltpu.make_async_copy(a_s, a_s, in_sem.at[4]).wait()

    def pair(x, y):
        return 0.25 * jnp.where(
            even, x + pltpu.roll(x, 127, 1), y + pltpu.roll(y, 1, 1)
        )

    def sunlit_of(m, b):
        def lat_row(i, k):
            return jnp.broadcast_to(lat_s[i, pl.ds(k, 1), :], (levels, 128))

        sl = jnp.where(even, lat_row(0, 2 * m), lat_row(0, 2 * m + 1))
        cl = jnp.where(even, lat_row(1, 2 * m), lat_row(1, 2 * m + 1))
        coslon = jnp.broadcast_to(lon_s[:, b * 128:(b + 1) * 128], (levels, 128))
        return jnp.maximum(sl * sin_dec + cl * cos_dec * coslon, 0.0)

    def prepare(m, _):
        for b in range(blocks):
            at = pl.ds(b * 128, 128)
            x = pair(
                m_s[4 * m, :, at] + m_s[4 * m + 1, :, at],
                m_s[4 * m + 2, :, at] + m_s[4 * m + 3, :, at],
            )
            depth = x
            for step in (1, 2, 4):
                depth = depth + jnp.where(sub >= step, pltpu.roll(depth, step, 0), 0.0)
            above = jnp.where(sub >= 1, pltpu.roll(depth, 1, 0), 0.0)
            total = jnp.broadcast_to(depth[levels - 1:levels, :], (levels, 128))
            slant = 1.0 / (sunlit_of(m, b) + MU_OFFSET)
            i = m * blocks + b
            tau[2 * i] = -LOG2E * (depth * slant)
            tau[2 * i + 1] = -LOG2E * (total * slant + DIFFUSE * (total - above))
        return 0

    lax.fori_loop(0, quads, prepare, 0)

    gpoints = absorb.shape[0]
    unroll = 2

    def fluxes(j, _):
        taus = [tau[j * 2 * CHUNK + i] for i in range(2 * CHUNK)]

        def gstep(h, sums):
            for e in range(unroll):
                a, w = absorb[h * unroll + e], weights[h * unroll + e]
                sums = tuple(s + w * jnp.exp2(a * x) for s, x in zip(sums, taus))
            return sums

        zeros = tuple(jnp.zeros((levels, 128), jnp.float32) for _ in taus)
        sums = lax.fori_loop(0, gpoints // unroll, gstep, zeros)
        for i in range(2 * CHUNK):
            fsum[j * 2 * CHUNK + i] = sums[i]
        return 0

    lax.fori_loop(0, quads * blocks // CHUNK, fluxes, 0)

    def weigh(h, sums):
        for e in range(2):
            sums = tuple(s + weights[8 * h + 4 * e + i] for i, s in enumerate(sums))
        return sums

    none = jnp.zeros((levels, 128), jnp.float32)
    part = lax.fori_loop(0, gpoints // 8, weigh, (none,) * 4)
    top = (part[0] + part[1]) + (part[2] + part[3])
    scale = HEAT_SCALE / gpoints

    def heat_row(m, _):
        for b in range(blocks):
            at = pl.ds(b * 128, 128)

            def alb_row(r):
                return jnp.broadcast_to(a_s[b, pl.ds(4 * m + r, 1), :], (levels, 128))

            surface = pair(alb_row(0) + alb_row(1), alb_row(2) + alb_row(3))
            i = m * blocks + b
            fd, fu = fsum[2 * i], fsum[2 * i + 1]
            fd_above = jnp.where(sub == 0, top, pltpu.roll(fd, 1, 0))
            fu_below = jnp.where(sub == levels - 1, fd, pltpu.roll(fu, levels - 1, 0))
            h = scale * sunlit_of(m, b) * ((fd_above - fd) - surface * (fu - fu_below))
            heat[2 * m, :, at] = jnp.where(even, h, pltpu.roll(h, 1, 1))
            heat[2 * m + 1, :, at] = jnp.where(even, pltpu.roll(h, 127, 1), h)
        return 0

    lax.fori_loop(0, quads, heat_row, 0)

    def halo(n, dst):
        first, count = msg_rows(n)

        @pl.when(t > 0)
        def _():
            recv_copy(0, n).wait()

        recv_copy(1, n).wait()
        if n == 1:
            @pl.when(t > 0)
            def _():
                e = recv[0, 0]
                d0[0] = d0[0] + e
                dst[2] = dst[2] - e
                acc[1] = acc[1] - e
            e = recv[1, 0]
            d0[rows - 1] = d0[rows - 1] + e
            dst[rows + 1] = dst[rows + 1] - e
            acc[rows] = acc[rows] - e

        for j in range(count):
            dst[rows + 2 + j] = recv[1, first + j] + keep[1, first + j]

        @pl.when(t > 0)
        def _():
            for j in range(count):
                dst[1 - j] = recv[0, first + j] + keep[0, first + j]

        @pl.when(t == 0)
        def _():
            dst[1] = zero_row
            if count > 1:
                dst[0] = dst[2]

        if n == 1:
            acc[0] = dst[1]
            acc[rows + 1] = dst[rows + 2]
        else:
            acc[0] = acc[0] + dst[1]
            acc[rows + 1] = acc[rows + 1] + dst[rows + 2]

    def first_row(r, _):
        x = p_s[r] - d0[r]
        pa[r + 2] = x
        acc[r + 1] = x
        return 0

    lax.fori_loop(0, rows, first_row, 0)
    cur, nxt = pa, pb
    halo(1, cur)
    for n in range(2, SUB + 1):
        def full_row(r, _, cur=cur, nxt=nxt):
            row_step(cur.at[r + 2], cur.at[r], cur.at[r + 4], d0.at[r], nxt.at[r + 2], acc.at[r + 1])
            return 0

        lax.fori_loop(0, rows, full_row, 0)
        cur, nxt = nxt, cur
        halo(n, cur)

    def final_row(r, _, cur=cur):
        x = acc[r + 1]
        u_s[r] = u_s[r] - half_c * (roll(x, -1) - roll(x, 1))
        v_s[r + 1] = v_s[r + 1] - half_c * (acc[r + 2] - acc[r])
        p_s[r] = cur[r + 2] + heat[r // 2]
        return 0

    lax.fori_loop(0, rows, final_row, 0)
    outs = [
        pltpu.make_async_copy(p_s, press_out, out_sem.at[0]),
        pltpu.make_async_copy(u_s, east_out, out_sem.at[1]),
        pltpu.make_async_copy(v_s.at[pl.ds(1, rows)], equator_out, out_sem.at[2]),
    ]
    for c in outs:
        c.start()
    for n in range(1, SUB + 1):
        down_copy(n).wait_send()

        @pl.when(t > 0)
        def _(n=n):
            up_copy(n).wait_send()
    for c in outs:
        c.wait()


def shards(tiles, east, equator, press, moist, alb, courant, sun, absorb, weights):
    _, levels, rows, cols = press.shape
    half_rows, quads, blocks = rows // 2, rows // 4, cols // 128
    row = lambda *lead: pltpu.VMEM(lead + (levels, cols), jnp.float32)
    out = jax.ShapeDtypeStruct((rows, levels, cols), jnp.float32)
    hbm = pl.BlockSpec(memory_space=pl.ANY)
    smem = pl.BlockSpec(memory_space=pltpu.SMEM)
    outs = pl.pallas_call(
        functools.partial(kernel, tiles),
        out_shape=(out, out, out),
        in_specs=[hbm] * 5 + [smem] * 4,
        out_specs=(hbm, hbm, hbm),
        scratch_shapes=[
            row(rows), row(rows + 2), row(rows), row(rows),
            pltpu.VMEM((blocks, rows, 128), jnp.float32),
            row(rows), row(rows + 4), row(rows + 4), row(rows + 2), row(half_rows),
            pltpu.VMEM((2, half_rows, 128), jnp.float32),
            pltpu.VMEM((1, cols), jnp.float32),
            pltpu.VMEM((2 * quads * blocks, levels, 128), jnp.float32),
            pltpu.VMEM((2 * quads * blocks, levels, 128), jnp.float32),
            row(2, OFF + rows), row(2, OFF + rows), row(2, OFF + rows),
            row(2, 2 * SUB), row(2, 2 * SUB), row(2, 2 * SUB),
            pltpu.SemaphoreType.DMA((5,)),
            pltpu.SemaphoreType.DMA((3,)),
            pltpu.SemaphoreType.DMA((2, SUB)),
            pltpu.SemaphoreType.DMA((2, SUB)),
        ],
        compiler_params=pltpu.CompilerParams(
            collective_id=0, has_side_effects=True, vmem_limit_bytes=60 * 1024 * 1024
        ),
        name="step",
    )(east, equator, press, moist, alb, courant, sun, absorb, weights)
    return tuple(jnp.swapaxes(o, 0, 1)[None] for o in outs)


def solution(mesh):
    field = P("group", None, "tile", None)
    return jax.shard_map(
        functools.partial(shards, mesh.shape["tile"]),
        mesh=mesh,
        in_specs=(field, field, field, field, P("group", "tile", None), P(), P(), P(), P()),
        out_specs=(field, field, field),
        check_vma=False,
    )
```
